32 devices in a mesh: rep: 8 (over z, core), fsdp: 4 (over y, x).
Axes of the slice: x: 2, y: 2, z: 4, core: 2. Of those that a mesh axis runs over, the one named last changes fastest.
Arguments:
- tokens: bfloat16 [512, 4096], P('fsdp', 'rep'), may hold values from -6 to 6
- grad_out: bfloat16 [512, 4096], P('fsdp', 'rep'), may hold values from -6 to 6
- w_gate: bfloat16 [4096, 24576], P('fsdp', 'rep'), may hold values from -0.125 to 0.125
- w_up: bfloat16 [4096, 24576], P('fsdp', 'rep'), may hold values from -0.125 to 0.125
- w_down: bfloat16 [24576, 4096], P('rep', 'fsdp'), may hold values from -0.0390625 to 0.0390625
Outputs:
- grad_tokens: bfloat16 [512, 4096], P('fsdp', 'rep')
- grad_gate: bfloat16 [4096, 24576], P('fsdp', 'rep')
- grad_up: bfloat16 [4096, 24576], P('fsdp', 'rep')
- grad_down: bfloat16 [24576, 4096], P('rep', 'fsdp')
The draws below stay inside these ranges and needn't reach their ends.
All inputs are finite; a program needn't handle non-finite values.
Results may differ from the reference program's by a relative error of at most 0.0049.
Values may be sent and summed in bfloat16 or wider, within the bound.
A program may use at most 192 MiB of HBM per device.

```python
import math
import jax
import jax.numpy as jnp
from jax import lax

D = 4096
FF = 24576
HB = 128
TOKENS = 512


def raised(entries, key, source, target, blocks, factor):
    owner, partner = [(jnp.arange(entries.shape[dim]) // (entries.shape[dim] // blocks)).reshape([-1 if axis == dim else 1 for axis in range(entries.ndim)]) for dim in (source, target)]
    chosen = jax.random.permutation(key, blocks)[partner]
    strong = (owner == chosen) | (owner == (partner + blocks // 2) % blocks)
    return jnp.where(strong, factor * entries, entries)


def block_levels(own_key, shape, cuts, smallest, high):
    def one(dim, blocks):
        draws = jax.random.uniform(jax.random.fold_in(jax.random.fold_in(own_key, 6), dim), (blocks,), jnp.float32, smallest / len(cuts), high / len(cuts))
        return jnp.repeat(jnp.exp(draws), shape[dim] // blocks).reshape((-1,) + (1,) * (len(shape) - dim - 1))

    gain = one(*cuts[0])
    for cut in cuts[1:]:
        gain = gain * one(*cut)
    return gain


def scatter_about(key, dims, deviation, reach, shards=(), kind=jnp.bfloat16):
    loudness = block_levels(key, dims, shards, -0.22, 0.18) if shards else 1.0
    array = jax.random.normal(key, dims, jnp.float32) * deviation * loudness
    return jnp.minimum(jnp.maximum(array, -reach), reach).astype(kind)


def noise_with(key, shape, deviation, bound, shards, heavy, kind=jnp.bfloat16):
    entries = deviation * jax.random.normal(key, shape, jnp.float32)
    if shards:
        entries = entries * block_levels(key, shape, shards, -0.22, 0.18)
    return jnp.clip(raised(entries, jax.random.fold_in(key, 3), *heavy), -bound, bound).astype(kind)


def setup_inputs(seed: int = 0) -> dict:
    key_list = jax.random.split(jax.random.key(seed), 6)
    return {
        "tokens": scatter_about(key_list[0], (TOKENS, D), 1.0, 6.0, ((0, 4), (1, 8))),
        "grad_out": scatter_about(key_list[1], (TOKENS, D), 1.0, 6.0, ((0, 4), (1, 8))),
        "w_gate": noise_with(key_list[2], (D, FF), D ** -0.5, 0.125, ((0, 4), (1, 8)), (1, 0, 8, 2.0)),
        "w_up": noise_with(key_list[3], (D, FF), D ** -0.5, 0.125, ((0, 4), (1, 8)), (1, 0, 8, 2.0)),
        "w_down": scatter_about(key_list[4], (FF, D), FF ** -0.5, 0.0390625, ((0, 8), (1, 4))),
    }


def hadamard(size):
    index = jnp.arange(size, dtype=jnp.int32)
    both = index[:, None] & index[None, :]
    parity = jnp.zeros((size, size), jnp.int32)
    for bit_pos in range(size.bit_length() - 1):
        parity = parity + (both >> bit_pos & 1)
    return (1 - 2 * (parity % 2)).astype(jnp.float32) / math.sqrt(size)

def reference(tokens, grad_out, w_gate, w_up, w_down):
    gate = jnp.dot(tokens, w_gate, preferred_element_type=jnp.float32)
    up = jnp.dot(tokens, w_up, preferred_element_type=jnp.float32)
    sig = jax.nn.sigmoid(gate)
    active = gate * sig
    hidden = (active * up).astype(jnp.bfloat16)
    d_hidden = jnp.dot(grad_out, w_down.T, preferred_element_type=jnp.float32)
    d_gate = (d_hidden * up * sig * (1.0 + gate * (1.0 - sig))).astype(jnp.bfloat16)
    d_up = (d_hidden * active).astype(jnp.bfloat16)
    grad_tokens = (jnp.dot(d_gate, w_gate.T, preferred_element_type=jnp.float32) + jnp.dot(d_up, w_up.T, preferred_element_type=jnp.float32)).astype(jnp.bfloat16)
    gw_gate = jnp.dot(tokens.T, d_gate, preferred_element_type=jnp.float32)
    gw_up = jnp.dot(tokens.T, d_up, preferred_element_type=jnp.float32)
    gw_down = jnp.dot(hidden.T, grad_out, preferred_element_type=jnp.float32)
    rotor = hadamard(HB)

    def rotate_rows(grad):
        blocks = grad.reshape(D // HB, HB, FF)
        return jnp.einsum('ij,bjf->bif', rotor, blocks, precision=lax.Precision.HIGHEST).reshape(D, FF).astype(jnp.bfloat16)
    blocks = gw_down.reshape(FF, D // HB, HB)
    grad_down = jnp.einsum('fbj,ij->fbi', blocks, rotor, precision=lax.Precision.HIGHEST).reshape(FF, D).astype(jnp.bfloat16)
    return (grad_tokens, rotate_rows(gw_gate), rotate_rows(gw_up), grad_down)
```

```python
import functools
import math

import jax
import jax.numpy as jnp
from jax import lax
from jax.experimental import pallas as pl
from jax.experimental.pallas import tpu as pltpu
from jax.sharding import PartitionSpec as P

HB = 128
BF16 = jnp.bfloat16
F32 = jnp.float32


def hadamard(size):
    index = jnp.arange(size, dtype=jnp.int32)
    both = index[:, None] & index[None, :]
    parity = jnp.zeros((size, size), jnp.int32)
    for bit_pos in range(size.bit_length() - 1):
        parity = parity + (both >> bit_pos & 1)
    return (1 - 2 * (parity % 2)).astype(F32) / math.sqrt(size)


def dot_dims(left, right, left_dim, right_dim, kind=F32):
    return lax.dot_general(
        left, right, (((left_dim,), (right_dim,)), ((), ())), preferred_element_type=kind
    )


def rotate_features(block):
    rows, width = block.shape
    parts = block.astype(F32).reshape(rows, width // HB, HB)
    turned = jnp.einsum("tbj,ij->tbi", parts, hadamard(HB), precision=lax.Precision.HIGHEST)
    return turned.reshape(rows, width).astype(BF16)


def gather_blocks(tokens, grad_out):
    both = jnp.stack([tokens, grad_out])
    full = lax.all_gather(both, "rep", axis=2, tiled=True)
    block = lax.all_to_all(full, "fsdp", split_axis=2, concat_axis=1, tiled=True)
    return block[0], block[1]


def activations(gate, up, d_hidden):
    sig = jax.nn.sigmoid(gate)
    active = gate * sig
    hidden = (active * up).astype(BF16)
    d_gate = (d_hidden * up * sig * (1.0 + gate * (1.0 - sig))).astype(BF16)
    d_up = (d_hidden * active).astype(BF16)
    return hidden, d_gate, d_up


def middle_plain(x_block, dy_block, w_gate, w_up, w_down):
    sums = [
        lax.psum_scatter(part, "fsdp", scatter_dimension=0, tiled=True)
        for part in (
            dot_dims(x_block, w_gate, 1, 0),
            dot_dims(x_block, w_up, 1, 0),
            dot_dims(dy_block, w_down, 1, 1),
        )
    ]
    own = activations(*sums)
    hidden, d_gate, d_up = [lax.all_gather(v, "fsdp", axis=0, tiled=True) for v in own]
    partial = dot_dims(d_gate, w_gate, 1, 1) + dot_dims(d_up, w_up, 1, 1)
    return hidden, d_gate, d_up, partial


MESH = pl.DeviceIdType.MESH
LAG = 2


def middle_kernel(
    n, x_ref, dy_ref, wg_hbm, wu_hbm, wd_hbm, hid_out, dg_out, du_out, total,
    w_pair, w_low, part, send1, recv1, send2, recv2, acts,
    w_sem, out_sem, ssem, rsem,
):
    chunk = w_low.shape[1]
    slots = part.shape[0]
    outs = (hid_out, dg_out, du_out)
    me = lax.axis_index("fsdp")
    y, x = me // 2, me % 2
    near_x, near_y = 2 * y + 1 - x, 2 * (1 - y) + x

    def span(c):
        return pl.ds(pl.multiple_of(c * chunk, chunk), chunk)

    def weights(c):
        return (
            pltpu.make_async_copy(wg_hbm.at[:, span(c)], w_pair.at[c, :, pl.ds(0, chunk)], w_sem.at[0, c]),
            pltpu.make_async_copy(wu_hbm.at[:, span(c)], w_pair.at[c, :, pl.ds(chunk, chunk)], w_sem.at[1, c]),
            pltpu.make_async_copy(wd_hbm.at[span(c), :], w_low.at[c], w_sem.at[2, c]),
        )

    def results(c):
        return [
            pltpu.make_async_copy(acts.at[c, :, k], outs[k].at[:, :, span(c)], out_sem.at[k, c])
            for k in range(3)
        ]

    def remote(stage, c):
        source, target, device = (
            (send1.at[c], recv1.at[c], near_x),
            (send2.at[c], recv2.at[c], near_y),
            (acts.at[c, me], acts.at[c, me], near_x),
            (acts.at[c, pl.ds(2 * y, 2)], acts.at[c, pl.ds(2 * y, 2)], near_y),
        )[stage]
        return pltpu.make_async_remote_copy(
            src_ref=source, dst_ref=target, send_sem=ssem.at[stage, c], recv_sem=rsem.at[stage, c],
            device_id={"fsdp": device}, device_id_type=MESH,
        )

    @pl.loop(0, n)
    def _(c):
        for copy in weights(c):
            copy.start()

    barrier = pltpu.get_barrier_semaphore()
    for device in (near_x, near_y):
        pl.semaphore_signal(barrier, inc=1, device_id={"fsdp": device}, device_id_type=MESH)
    pl.semaphore_wait(barrier, 2)

    total[...] = jnp.zeros_like(total)

    @pl.loop(0, n + 4 * LAG)
    def _(step):
        @pl.when(step < n)
        def _():
            c = step
            slot = lax.rem(c, slots)
            for copy in weights(c):
                copy.wait()
            pair = jnp.dot(x_ref[...], w_pair[c], preferred_element_type=F32)
            part[slot, :, 0] = pair[:, :chunk].reshape(4, -1, chunk)
            part[slot, :, 1] = pair[:, chunk:].reshape(4, -1, chunk)
            part[slot, :, 2] = dot_dims(dy_ref[...], w_low[c], 1, 1).reshape(4, -1, chunk)
            for row in range(2):
                send1[c, row] = part[slot, 2 * row + 1 - x].astype(BF16)
            remote(0, c).start()

        @pl.when((step >= LAG) & (step < n + LAG))
        def _():
            c = step - LAG
            slot = lax.rem(c, slots)
            remote(0, c).wait_recv()
            send2[c] = (part[slot, near_y] + recv1[c, 1 - y].astype(F32)).astype(BF16)
            remote(1, c).start()

        @pl.when((step >= 2 * LAG) & (step < n + 2 * LAG))
        def _():
            c = step - 2 * LAG
            slot = lax.rem(c, slots)
            remote(1, c).wait_recv()
            sums = [
                part[slot, me, k] + recv1[c, y, k].astype(F32) + recv2[c, k].astype(F32)
                for k in range(3)
            ]
            for k, value in enumerate(activations(*sums)):
                acts[c, me, k] = value
            remote(2, c).start()

        @pl.when((step >= 3 * LAG) & (step < n + 3 * LAG))
        def _():
            c = step - 3 * LAG
            remote(2, c).wait_recv()
            remote(3, c).start()

        @pl.when(step >= 4 * LAG)
        def _():
            c = step - 4 * LAG
            remote(3, c).wait_recv()
            for copy in results(c):
                copy.start()
            pair = jnp.concatenate(
                [acts[c, :, 1].reshape(-1, chunk), acts[c, :, 2].reshape(-1, chunk)], axis=1
            )
            total[...] += dot_dims(pair, w_pair[c], 1, 1)
            for stage in range(4):
                remote(stage, c).wait_send()

    @pl.loop(0, n)
    def _(c):
        for copy in results(c):
            copy.wait()


def middle_fused(x_block, dy_block, w_gate, w_up, w_down):
    tokens, width = x_block.shape
    units = w_gate.shape[1]
    chunk = 128
    n, rows = units // chunk, tokens // 4
    whole, anywhere = pl.BlockSpec(memory_space=pltpu.VMEM), pl.BlockSpec(memory_space=pl.ANY)
    wide = jax.ShapeDtypeStruct((4, rows, units), BF16)
    *acts, total = pl.pallas_call(
        functools.partial(middle_kernel, n),
        out_shape=(wide, wide, wide, jax.ShapeDtypeStruct((tokens, width), F32)),
        in_specs=[whole, whole, anywhere, anywhere, anywhere],
        out_specs=(anywhere, anywhere, anywhere, whole),
        scratch_shapes=[
            pltpu.VMEM((n, width, 2 * chunk), BF16),
            pltpu.VMEM((n, chunk, width), BF16),
            pltpu.VMEM((2 * LAG + 1, 4, 3, rows, chunk), F32),
            pltpu.VMEM((n, 2, 3, rows, chunk), BF16),
            pltpu.VMEM((n, 2, 3, rows, chunk), BF16),
            pltpu.VMEM((n, 3, rows, chunk), BF16),
            pltpu.VMEM((n, 3, rows, chunk), BF16),
            pltpu.VMEM((n, 4, 3, rows, chunk), BF16),
            pltpu.SemaphoreType.DMA((3, n)),
            pltpu.SemaphoreType.DMA((3, n)),
            pltpu.SemaphoreType.DMA((4, n)),
            pltpu.SemaphoreType.DMA((4, n)),
        ],
        compiler_params=pltpu.CompilerParams(
            collective_id=0, has_side_effects=True, vmem_limit_bytes=60 * 2**20
        ),
        cost_estimate=pl.CostEstimate(
            flops=10 * tokens * width * units, bytes_accessed=12 * width * units, transcendentals=0
        ),
    )(x_block, dy_block, w_gate, w_up, w_down)
    return (*[v.reshape(tokens, units) for v in acts], total)


def scatter_tokens(partial, n_rep, n_fsdp):
    rows, width = partial.shape
    halves = n_rep // n_fsdp
    pieces = partial.reshape(n_fsdp, rows // n_fsdp, halves, width // halves)
    pieces = pieces.transpose(0, 2, 1, 3).reshape(n_rep, rows // n_fsdp, width // halves)
    piece = lax.psum_scatter(pieces, "rep", scatter_dimension=0, tiled=False)
    pairs = []
    for f in range(n_fsdp):
        for r in range(n_rep):
            t, h = divmod(r, halves)
            pairs.append((r * n_fsdp + f, (f * halves + h) * n_fsdp + t))
    return lax.ppermute(piece.astype(BF16), ("rep", "fsdp"), pairs)


def solution(mesh):
    n_rep, n_fsdp = mesh.shape["rep"], mesh.shape["fsdp"]

    def body(tokens, grad_out, w_gate, w_up, w_down):
        x_block, dy_block = gather_blocks(tokens, grad_out)
        middle = middle_fused if n_fsdp == 4 else middle_plain
        hidden, d_gate, d_up, partial = middle(x_block, dy_block, w_gate, w_up, w_down)
        grad_tokens = scatter_tokens(partial, n_rep, n_fsdp)
        x_turned, dy_turned = rotate_features(x_block), rotate_features(dy_block)
        return (
            grad_tokens,
            dot_dims(x_turned, d_gate, 0, 0).astype(BF16),
            dot_dims(x_turned, d_up, 0, 0).astype(BF16),
            dot_dims(hidden, dy_turned, 0, 0).astype(BF16),
        )

    return jax.shard_map(
        body,
        mesh=mesh,
        in_specs=(P("fsdp", "rep"),) * 4 + (P("rep", "fsdp"),),
        out_specs=(P("fsdp", "rep"),) * 3 + (P("rep", "fsdp"),),
        check_vma=False,
    )
```

```python
import functools
import math

import jax
import jax.numpy as jnp
from jax import lax
from jax.experimental import pallas as pl
from jax.experimental.pallas import tpu as pltpu
from jax.sharding import PartitionSpec as P

HB = 128
BF16 = jnp.bfloat16
F32 = jnp.float32


def hadamard(size):
    index = jnp.arange(size, dtype=jnp.int32)
    both = index[:, None] & index[None, :]
    parity = jnp.zeros((size, size), jnp.int32)
    for bit_pos in range(size.bit_length() - 1):
        parity = parity + (both >> bit_pos & 1)
    return (1 - 2 * (parity % 2)).astype(F32) / math.sqrt(size)


def dot_dims(left, right, left_dim, right_dim, kind=F32):
    return lax.dot_general(
        left, right, (((left_dim,), (right_dim,)), ((), ())), preferred_element_type=kind
    )


def rotate_features(block):
    rows, width = block.shape
    parts = block.astype(F32).reshape(rows, width // HB, HB)
    turned = jnp.einsum("tbj,ij->tbi", parts, hadamard(HB), precision=lax.Precision.HIGHEST)
    return turned.reshape(rows, width).astype(BF16)


def gather_blocks(tokens, grad_out):
    both = jnp.stack([tokens, grad_out])
    full = lax.all_gather(both, "rep", axis=2, tiled=True)
    block = lax.all_to_all(full, "fsdp", split_axis=2, concat_axis=1, tiled=True)
    return block[0], block[1]


def activations(gate, up, d_hidden):
    sig = jax.nn.sigmoid(gate)
    active = gate * sig
    hidden = (active * up).astype(BF16)
    d_gate = (d_hidden * up * sig * (1.0 + gate * (1.0 - sig))).astype(BF16)
    d_up = (d_hidden * active).astype(BF16)
    return hidden, d_gate, d_up


def middle_plain(x_block, dy_block, w_gate, w_up, w_down):
    sums = [
        lax.psum_scatter(part, "fsdp", scatter_dimension=0, tiled=True)
        for part in (
            dot_dims(x_block, w_gate, 1, 0),
            dot_dims(x_block, w_up, 1, 0),
            dot_dims(dy_block, w_down, 1, 1),
        )
    ]
    own = activations(*sums)
    hidden, d_gate, d_up = [lax.all_gather(v, "fsdp", axis=0, tiled=True) for v in own]
    partial = dot_dims(d_gate, w_gate, 1, 1) + dot_dims(d_up, w_up, 1, 1)
    return hidden, d_gate, d_up, partial


def scatter_tokens(partial, n_rep, n_fsdp):
    rows, width = partial.shape
    halves = n_rep // n_fsdp
    pieces = partial.reshape(n_fsdp, rows // n_fsdp, halves, width // halves)
    pieces = pieces.transpose(0, 2, 1, 3).reshape(n_rep, rows // n_fsdp, width // halves)
    piece = lax.psum_scatter(pieces, "rep", scatter_dimension=0, tiled=False)
    pairs = []
    for f in range(n_fsdp):
        for r in range(n_rep):
            t, h = divmod(r, halves)
            pairs.append((r * n_fsdp + f, (f * halves + h) * n_fsdp + t))
    return lax.ppermute(piece.astype(BF16), ("rep", "fsdp"), pairs)


MESH = pl.DeviceIdType.MESH
LAG = 2


def fused_kernel(
    n, tok_ref, go_ref, sign_ref, wg_hbm, wu_hbm, wd_hbm,
    hid_out, dg_out, du_out, gt_out, xt_out, dyt_out,
    w_pair, w_low, part, send1, recv1, send2, recv2, acts, hid,
    zbuf, gath, x_ref, dy_ref, total, e1recv, e2send, e2recv, e3send, e3recv,
    w_sem, out_sem, ssem, rsem, gs_sem, gr_sem, hs_sem, hr_sem, es_sem, er_sem,
):
    chunk = w_low.shape[1]
    slots = part.shape[0]
    rows, feats = tok_ref.shape
    me, rep = lax.axis_index("fsdp"), lax.axis_index("rep")
    z, h = rep // 2, rep % 2
    sibling = rep + 1 - 2 * h
    y, x = me // 2, me % 2
    near_x, near_y, far = 2 * y + 1 - x, 2 * (1 - y) + x, 3 - me

    def span(c, size):
        return pl.ds(pl.multiple_of(c * size, size), size)

    def send(source, target, send_sem, recv_sem, fsdp, to):
        return pltpu.make_async_remote_copy(
            src_ref=source, dst_ref=target, send_sem=send_sem, recv_sem=recv_sem,
            device_id={"rep": to, "fsdp": fsdp}, device_id_type=MESH,
        )

    def weights(c):
        columns = span(c, chunk)
        return (
            pltpu.make_async_copy(wg_hbm.at[:, columns], w_pair.at[c, :, pl.ds(0, chunk)], w_sem.at[0, c]),
            pltpu.make_async_copy(wu_hbm.at[:, columns], w_pair.at[c, :, pl.ds(chunk, chunk)], w_sem.at[1, c]),
            pltpu.make_async_copy(wd_hbm.at[columns, :], w_low.at[c], w_sem.at[2, c]),
        )

    def results(c):
        return [
            pltpu.make_async_copy(acts.at[c, :, k], out.at[:, :, span(c, chunk)], out_sem.at[k, c])
            for k, out in enumerate((dg_out, du_out))
        ]

    def hidden_result(c):
        return pltpu.make_async_copy(hid.at[c], hid_out.at[:, :, span(c, chunk)], out_sem.at[2, c])

    def partners(c):
        odd = lax.rem(c, 2)
        first = near_x * (1 - odd) + near_y * odd
        return first, near_x + near_y - first

    def remote(stage, c):
        first, second = partners(c)
        source, target, device = (
            (send1.at[c, 0], recv1.at[c, 0], first),
            (send1.at[c, 1], recv1.at[c, 1], first),
            (send2.at[c], recv2.at[c], second),
            (acts.at[c, me], acts.at[c, me], first),
            (acts.at[c, me], acts.at[c, me], second),
            (acts.at[c, first], acts.at[c, first], second),
        )[stage]
        return send(source, target, ssem.at[stage, c], rsem.at[stage, c], device, rep)

    @pl.loop(0, n)
    def _(c):
        for copy in weights(c):
            copy.start()

    zbuf[z, 0] = tok_ref[...]
    zbuf[z, 1] = go_ref[...]

    barrier = pltpu.get_barrier_semaphore()

    def greet(fsdp, to):
        pl.semaphore_signal(
            barrier, inc=1, device_id={"rep": to, "fsdp": fsdp}, device_id_type=MESH
        )

    for k in range(1, 4):
        greet(me, 2 * ((z + k) % 4) + h)
        greet((me + k) % 4, rep)
    greet(me, sibling)

    @pl.when(me != z)
    def _():
        greet(z, 2 * me + h)

    pl.semaphore_wait(barrier, 7 + jnp.where(me != z, 1, 0))

    def along_z(k):
        return send(zbuf.at[z], zbuf.at[z], gs_sem.at[0, k], gr_sem.at[0, z], me, 2 * ((z + k) % 4) + h)

    def to_owner(block):
        return send(zbuf.at[block], gath.at[me, h], gs_sem.at[1, block], gr_sem.at[1, me], block, rep)

    def to_core(owner):
        return send(gath.at[owner, h], gath.at[owner, h], gs_sem.at[2, owner], gr_sem.at[2, owner], me, sibling)

    def arrived(target, sem):
        pltpu.make_async_copy(target, target, sem).wait()

    def pass_on(block):
        @pl.when(block != me)
        def _():
            to_owner(block).start()

        @pl.when(block == me)
        def _():
            gath[me, h] = zbuf[block]
            to_core(me).start()

    for k in (1, 3, 2):
        along_z(k).start()
    pass_on(z)
    for k in (1, 3, 2):
        block = (z + k) % 4
        arrived(zbuf.at[block], gr_sem.at[0, block])
        pass_on(block)
    for k in (1, 2, 3):
        owner = (me + k) % 4
        arrived(gath.at[owner, h], gr_sem.at[1, owner])
        to_core(owner).start()
    for k in range(4):
        owner = (me + k) % 4
        arrived(gath.at[owner, 1 - h], gr_sem.at[2, owner])
    for owner in range(4):
        for half in range(2):
            place = (pl.ds(owner * rows, rows), pl.ds(half * feats, feats))
            x_ref[place] = gath[owner, half, 0]
            dy_ref[place] = gath[owner, half, 1]

    total[...] = jnp.zeros_like(total)

    @pl.loop(0, n + 4 * LAG)
    def _(step):
        @pl.when(step < n)
        def _():
            c = step
            slot = lax.rem(c, slots)
            for copy in weights(c):
                copy.wait()
            pair = jnp.dot(x_ref[...], w_pair[c], preferred_element_type=F32)
            part[slot, :, 0] = pair[:, :chunk].reshape(4, -1, chunk)
            part[slot, :, 1] = pair[:, chunk:].reshape(4, -1, chunk)
            part[slot, :, 2] = dot_dims(dy_ref[...], w_low[c], 1, 1).reshape(4, -1, chunk)
            first, _ = partners(c)
            send1[c, 0] = part[slot, far].astype(BF16)
            remote(0, c).start()
            send1[c, 1] = part[slot, first].astype(BF16)
            remote(1, c).start()

        @pl.when((step >= LAG) & (step < n + LAG))
        def _():
            c = step - LAG
            slot = lax.rem(c, slots)
            _, second = partners(c)
            remote(0, c).wait_recv()
            send2[c] = (part[slot, second] + recv1[c, 0].astype(F32)).astype(BF16)
            remote(2, c).start()

        @pl.when((step >= 2 * LAG) & (step < n + 2 * LAG))
        def _():
            c = step - 2 * LAG
            slot = lax.rem(c, slots)
            remote(1, c).wait_recv()
            remote(2, c).wait_recv()
            sums = [
                part[slot, me, k] + recv1[c, 1, k].astype(F32) + recv2[c, k].astype(F32)
                for k in range(3)
            ]
            hidden, d_gate, d_up = activations(*sums)
            acts[c, me, 0] = d_gate
            acts[c, me, 1] = d_up
            remote(3, c).start()
            remote(4, c).start()
            hid[c, me] = hidden

        @pl.when((step >= 3 * LAG) & (step < n + 3 * LAG))
        def _():
            c = step - 3 * LAG
            remote(3, c).wait_recv()
            remote(5, c).start()

        @pl.when(step >= 4 * LAG)
        def _():
            c = step - 4 * LAG
            remote(4, c).wait_recv()
            remote(5, c).wait_recv()
            for copy in results(c):
                copy.start()
            pair = jnp.concatenate(
                [acts[c, :, 0].reshape(-1, chunk), acts[c, :, 1].reshape(-1, chunk)], axis=1
            )
            total[...] += dot_dims(pair, w_pair[c], 1, 1)
            for stage in range(6):
                remote(stage, c).wait_send()

    low, high = pl.ds(0, n // 2), pl.ds(n // 2, n - n // 2)

    def hidden_copy(k):
        part_of, owner, device = (
            (low, me, near_x), (high, me, near_y), (high, me, near_x), (low, me, near_y),
            (low, near_x, near_y), (high, near_y, near_x),
        )[k]
        block = hid.at[part_of, owner]
        return send(block, block, hs_sem.at[k], hr_sem.at[k], device, rep)

    for k in range(4):
        hidden_copy(k).start()

    def half(core):
        return pl.ds(pl.multiple_of(core * feats, feats), feats)

    fold = send(total.at[:, half(1 - h)], e1recv, es_sem.at[0], er_sem.at[0], me, sibling)
    fold.start()
    scale = 1.0 / math.sqrt(HB)
    for source, target in ((x_ref, xt_out), (dy_ref, dyt_out)):
        for b in range(source.shape[1] // HB):
            columns = pl.ds(b * HB, HB)
            turned = jnp.dot(source[:, columns], sign_ref[...], preferred_element_type=F32)
            target[:, columns] = (turned * scale).astype(BF16)
    fold.wait()
    for t in range(4):
        block = pl.ds(t * rows, rows)
        e1recv[block, :] = e1recv[block, :] + total[block, half(h)]
        e2send[t] = e1recv[block, :].astype(BF16)

    def piece(k):
        t = (z + k) % 4
        return send(e2send.at[t], e2recv.at[z], es_sem.at[k], er_sem.at[1 + z], me, 2 * t + h)

    for k in (2, 1, 3):
        piece(k).start()
    hidden_copy(0).wait_recv()
    hidden_copy(4).start()
    hidden_copy(1).wait_recv()
    hidden_copy(5).start()
    for k in (1, 3, 2):
        source = (z + k) % 4
        arrived(e2recv.at[source], er_sem.at[1 + source])
    mine = e1recv[span(z, rows), :]
    for k in range(1, 4):
        mine = mine + e2recv[(z + k) % 4].astype(F32)
    e3send[...] = mine.astype(BF16)
    swap = send(e3send, e3recv, es_sem.at[4], er_sem.at[5], z, 2 * me + h)

    @pl.when(me != z)
    def _():
        swap.start()
        swap.wait()
        gt_out[...] = e3recv[...]

    @pl.when(me == z)
    def _():
        gt_out[...] = e3send[...]

    for k in range(2, 6):
        hidden_copy(k).wait_recv()

    @pl.loop(0, n)
    def _(c):
        hidden_result(c).start()

    for k in range(6):
        hidden_copy(k).wait_send()
    for k in range(1, 4):
        piece(k).wait_send()
        along_z(k).wait_send()
    for block in range(4):
        @pl.when(block != me)
        def _():
            to_owner(block).wait_send()

        to_core(block).wait_send()

    @pl.loop(0, n)
    def _(c):
        for copy in results(c):
            copy.wait()
        hidden_result(c).wait()


def fused(tokens, grad_out, w_gate, w_up, w_down):
    rows, feats = tokens.shape
    width, units = w_gate.shape
    chunk = 128
    n, count = units // chunk, 4 * rows
    signs = (hadamard(HB) * math.sqrt(HB)).astype(BF16)
    whole, anywhere = pl.BlockSpec(memory_space=pltpu.VMEM), pl.BlockSpec(memory_space=pl.ANY)
    wide = jax.ShapeDtypeStruct((4, rows, units), BF16)
    turned = jax.ShapeDtypeStruct((count, width), BF16)
    dma = pltpu.SemaphoreType.DMA
    hidden, d_gate, d_up, grad_tokens, x_turned, dy_turned = pl.pallas_call(
        functools.partial(fused_kernel, n),
        out_shape=(wide, wide, wide, jax.ShapeDtypeStruct((rows, feats), BF16), turned, turned),
        in_specs=[whole] * 3 + [anywhere] * 3,
        out_specs=(anywhere,) * 3 + (whole,) * 3,
        scratch_shapes=[
            pltpu.VMEM((n, width, 2 * chunk), BF16),
            pltpu.VMEM((n, chunk, width), BF16),
            pltpu.VMEM((2 * LAG + 1, 4, 3, rows, chunk), F32),
            pltpu.VMEM((n, 2, 3, rows, chunk), BF16),
            pltpu.VMEM((n, 2, 3, rows, chunk), BF16),
            pltpu.VMEM((n, 3, rows, chunk), BF16),
            pltpu.VMEM((n, 3, rows, chunk), BF16),
            pltpu.VMEM((n, 4, 2, rows, chunk), BF16),
            pltpu.VMEM((n, 4, rows, chunk), BF16),
            pltpu.VMEM((4, 2, rows, feats), BF16),
            pltpu.VMEM((4, 2, 2, rows, feats), BF16),
            pltpu.VMEM((count, width), BF16),
            pltpu.VMEM((count, width), BF16),
            pltpu.VMEM((count, width), F32),
            pltpu.VMEM((count, feats), F32),
            pltpu.VMEM((4, rows, feats), BF16),
            pltpu.VMEM((4, rows, feats), BF16),
            pltpu.VMEM((rows, feats), BF16),
            pltpu.VMEM((rows, feats), BF16),
            dma((3, n)), dma((3, n)), dma((6, n)), dma((6, n)),
            dma((3, 4)), dma((3, 4)), dma((6,)), dma((6,)), dma((5,)), dma((6,)),
        ],
        compiler_params=pltpu.CompilerParams(
            collective_id=0, has_side_effects=True, vmem_limit_bytes=62 * 2**20
        ),
        cost_estimate=pl.CostEstimate(
            flops=10 * count * width * units, bytes_accessed=12 * width * units, transcendentals=0
        ),
    )(tokens, grad_out, signs, w_gate, w_up, w_down)
    flat = [v.reshape(count, units) for v in (hidden, d_gate, d_up)]
    return (*flat, grad_tokens, x_turned, dy_turned)


def plain(n_rep, n_fsdp, tokens, grad_out, w_gate, w_up, w_down):
    x_block, dy_block = gather_blocks(tokens, grad_out)
    hidden, d_gate, d_up, partial = middle_plain(x_block, dy_block, w_gate, w_up, w_down)
    grad_tokens = scatter_tokens(partial, n_rep, n_fsdp)
    return hidden, d_gate, d_up, grad_tokens, rotate_features(x_block), rotate_features(dy_block)


def solution(mesh):
    n_rep, n_fsdp = mesh.shape["rep"], mesh.shape["fsdp"]
    whole = fused if (n_rep, n_fsdp) == (8, 4) else functools.partial(plain, n_rep, n_fsdp)

    def body(tokens, grad_out, w_gate, w_up, w_down):
        hidden, d_gate, d_up, grad_tokens, x_turned, dy_turned = whole(
            tokens, grad_out, w_gate, w_up, w_down
        )
        return (
            grad_tokens,
            dot_dims(x_turned, d_gate, 0, 0).astype(BF16),
            dot_dims(x_turned, d_up, 0, 0).astype(BF16),
            dot_dims(hidden, dy_turned, 0, 0).astype(BF16),
        )

    return jax.shard_map(
        body,
        mesh=mesh,
        in_specs=(P("fsdp", "rep"),) * 4 + (P("rep", "fsdp"),),
        out_specs=(P("fsdp", "rep"),) * 3 + (P("rep", "fsdp"),),
        check_vma=False,
    )
```

```python
import functools
import math

import jax
import jax.numpy as jnp
from jax import lax
from jax.experimental import pallas as pl
from jax.experimental.pallas import tpu as pltpu
from jax.sharding import PartitionSpec as P

HB = 128
BF16 = jnp.bfloat16
F32 = jnp.float32


def hadamard(size):
    index = jnp.arange(size, dtype=jnp.int32)
    both = index[:, None] & index[None, :]
    parity = jnp.zeros((size, size), jnp.int32)
    for bit_pos in range(size.bit_length() - 1):
        parity = parity + (both >> bit_pos & 1)
    return (1 - 2 * (parity % 2)).astype(F32) / math.sqrt(size)


def dot_dims(left, right, left_dim, right_dim, kind=F32):
    return lax.dot_general(
        left, right, (((left_dim,), (right_dim,)), ((), ())), preferred_element_type=kind
    )


def rotate_features(block):
    rows, width = block.shape
    parts = block.astype(F32).reshape(rows, width // HB, HB)
    turned = jnp.einsum("tbj,ij->tbi", parts, hadamard(HB), precision=lax.Precision.HIGHEST)
    return turned.reshape(rows, width).astype(BF16)


def gather_blocks(tokens, grad_out):
    both = jnp.stack([tokens, grad_out])
    full = lax.all_gather(both, "rep", axis=2, tiled=True)
    block = lax.all_to_all(full, "fsdp", split_axis=2, concat_axis=1, tiled=True)
    return block[0], block[1]


def activations(gate, up, d_hidden):
    sig = jax.nn.sigmoid(gate)
    active = gate * sig
    hidden = (active * up).astype(BF16)
    d_gate = (d_hidden * up * sig * (1.0 + gate * (1.0 - sig))).astype(BF16)
    d_up = (d_hidden * active).astype(BF16)
    return hidden, d_gate, d_up


def middle_plain(x_block, dy_block, w_gate, w_up, w_down):
    sums = [
        lax.psum_scatter(part, "fsdp", scatter_dimension=0, tiled=True)
        for part in (
            dot_dims(x_block, w_gate, 1, 0),
            dot_dims(x_block, w_up, 1, 0),
            dot_dims(dy_block, w_down, 1, 1),
        )
    ]
    own = activations(*sums)
    hidden, d_gate, d_up = [lax.all_gather(v, "fsdp", axis=0, tiled=True) for v in own]
    partial = dot_dims(d_gate, w_gate, 1, 1) + dot_dims(d_up, w_up, 1, 1)
    return hidden, d_gate, d_up, partial


def scatter_tokens(partial, n_rep, n_fsdp):
    rows, width = partial.shape
    halves = n_rep // n_fsdp
    pieces = partial.reshape(n_fsdp, rows // n_fsdp, halves, width // halves)
    pieces = pieces.transpose(0, 2, 1, 3).reshape(n_rep, rows // n_fsdp, width // halves)
    piece = lax.psum_scatter(pieces, "rep", scatter_dimension=0, tiled=False)
    pairs = []
    for f in range(n_fsdp):
        for r in range(n_rep):
            t, h = divmod(r, halves)
            pairs.append((r * n_fsdp + f, (f * halves + h) * n_fsdp + t))
    return lax.ppermute(piece.astype(BF16), ("rep", "fsdp"), pairs)


MESH = pl.DeviceIdType.MESH
LAG = 2


def fused_kernel(
    n, tok_ref, go_ref, sign_ref, wg_hbm, wu_hbm, wd_hbm,
    hid_out, dg_out, du_out, gt_out, xt_out, dyt_out,
    w_pair, w_low, part, send1, recv1, send2, recv2, acts, hid,
    zbuf, gath, x_ref, dy_ref, total, e1recv, e2send, e2recv, e3send, e3recv,
    w_sem, out_sem, ssem, rsem, gs_sem, gr_sem, hs_sem, hr_sem, es_sem, er_sem,
):
    chunk = w_low.shape[1]
    slots = part.shape[0]
    rows, feats = tok_ref.shape
    me, rep = lax.axis_index("fsdp"), lax.axis_index("rep")
    z, h = rep // 2, rep % 2
    sibling = rep + 1 - 2 * h
    y, x = me // 2, me % 2
    near_x, near_y, far = 2 * y + 1 - x, 2 * (1 - y) + x, 3 - me

    def span(c, size):
        return pl.ds(pl.multiple_of(c * size, size), size)

    def send(source, target, send_sem, recv_sem, fsdp, to):
        return pltpu.make_async_remote_copy(
            src_ref=source, dst_ref=target, send_sem=send_sem, recv_sem=recv_sem,
            device_id={"rep": to, "fsdp": fsdp}, device_id_type=MESH,
        )

    def weights(c):
        columns = span(c, chunk)
        return (
            pltpu.make_async_copy(wg_hbm.at[:, columns], w_pair.at[c, :, pl.ds(0, chunk)], w_sem.at[0, c]),
            pltpu.make_async_copy(wu_hbm.at[:, columns], w_pair.at[c, :, pl.ds(chunk, chunk)], w_sem.at[1, c]),
            pltpu.make_async_copy(wd_hbm.at[columns, :], w_low.at[c], w_sem.at[2, c]),
        )

    def results(c):
        return [
            pltpu.make_async_copy(acts.at[c, :, k], out.at[:, :, span(c, chunk)], out_sem.at[k, c])
            for k, out in enumerate((dg_out, du_out))
        ]

    def hidden_result(c):
        return pltpu.make_async_copy(hid.at[c], hid_out.at[:, :, span(c, chunk)], out_sem.at[2, c])

    def partners(c):
        odd = lax.rem(c, 2)
        first = near_x * (1 - odd) + near_y * odd
        return first, near_x + near_y - first

    def remote(stage, c):
        first, second = partners(c)
        source, target, device = (
            (send1.at[c, 0], recv1.at[c, 0], first),
            (send1.at[c, 1], recv1.at[c, 1], first),
            (send2.at[c], recv2.at[c], second),
            (acts.at[c, me], acts.at[c, me], first),
            (acts.at[c, me], acts.at[c, me], second),
            (acts.at[c, first], acts.at[c, first], second),
        )[stage]
        return send(source, target, ssem.at[stage, c], rsem.at[stage, c], device, rep)

    @pl.loop(0, n)
    def _(c):
        for copy in weights(c):
            copy.start()

    zbuf[z, 0] = tok_ref[...]
    zbuf[z, 1] = go_ref[...]

    barrier = pltpu.get_barrier_semaphore()

    def greet(fsdp, to):
        pl.semaphore_signal(
            barrier, inc=1, device_id={"rep": to, "fsdp": fsdp}, device_id_type=MESH
        )

    for k in range(1, 4):
        greet(me, 2 * ((z + k) % 4) + h)
        greet((me + k) % 4, rep)
    greet(me, sibling)

    @pl.when(me != z)
    def _():
        greet(z, 2 * me + h)

    pl.semaphore_wait(barrier, 7 + jnp.where(me != z, 1, 0))

    total[...] = jnp.zeros_like(total)

    def upward(block, kind):
        here = zbuf.at[block, kind]
        return send(here, here, gs_sem.at[0, kind, block], gr_sem.at[0, kind, block], me, rep + 2)

    def downward(block, kind):
        here = zbuf.at[block, kind]
        return send(here, here, gs_sem.at[1, kind, block], gr_sem.at[0, kind, block], me, rep - 2)

    def to_owner(block, kind):
        return send(
            zbuf.at[block, kind], gath.at[me, h, kind],
            gs_sem.at[2, kind, block], gr_sem.at[1, kind, me], block, rep,
        )

    def to_core(owner, kind):
        here = gath.at[owner, h, kind]
        return send(here, here, gs_sem.at[3, kind, owner], gr_sem.at[2, kind, owner], me, sibling)

    def arrived(target, sem):
        pltpu.make_async_copy(target, target, sem).wait()

    def pass_on(block, kind):
        @pl.when(block != me)
        def _():
            to_owner(block, kind).start()

        @pl.when(block == me)
        def _():
            gath[me, h, kind] = zbuf[block, kind]
            to_core(me, kind).start()

    def relay(block, kind, go, copy):
        @pl.when(go)
        def _():
            copy(block, kind).start()

    for kind in range(2):
        relay(z, kind, z < 3, upward)
        relay(z, kind, z > 0, downward)
    for kind in range(2):
        pass_on(z, kind)
    for k in range(1, 4):
        for kind in range(2):
            for block, there, go, copy in (
                (z - k, z >= k, z < 3, upward), (z + k, z + k < 4, z > 0, downward),
            ):
                @pl.when(there)
                def _(block=block, kind=kind, go=go, copy=copy):
                    arrived(zbuf.at[block, kind], gr_sem.at[0, kind, block])
                    relay(block, kind, go, copy)
                    pass_on(block, kind)

    for kind in range(2):
        for k in range(1, 4):
            owner = (me + k) % 4
            arrived(gath.at[owner, h, kind], gr_sem.at[1, kind, owner])
            to_core(owner, kind).start()
    for kind, target in enumerate((x_ref, dy_ref)):
        for k in range(4):
            owner = (me + k) % 4
            arrived(gath.at[owner, 1 - h, kind], gr_sem.at[2, kind, owner])
        for owner in range(4):
            for side in range(2):
                place = (pl.ds(owner * rows, rows), pl.ds(side * feats, feats))
                target[place] = gath[owner, side, kind]

    low, high = pl.ds(0, n // 2), pl.ds(n // 2, n - n // 2)

    def hidden_copy(k):
        part_of, owner, device = (
            (low, me, near_x), (high, me, near_y), (high, me, near_x), (low, me, near_y),
            (low, near_x, near_y), (high, near_y, near_x),
        )[k]
        block = hid.at[part_of, owner]
        return send(block, block, hs_sem.at[k], hr_sem.at[k], device, rep)

    @pl.loop(0, n + 4 * LAG)
    def _(step):
        @pl.when(step < n)
        def _():
            c = step
            slot = lax.rem(c, slots)
            for copy in weights(c):
                copy.wait()
            pair = jnp.dot(x_ref[...], w_pair[c], preferred_element_type=F32)
            part[slot, :, 0] = pair[:, :chunk].reshape(4, -1, chunk)
            part[slot, :, 1] = pair[:, chunk:].reshape(4, -1, chunk)
            part[slot, :, 2] = dot_dims(dy_ref[...], w_low[c], 1, 1).reshape(4, -1, chunk)
            first, _ = partners(c)
            send1[c, 0] = part[slot, far].astype(BF16)
            remote(0, c).start()
            send1[c, 1] = part[slot, first].astype(BF16)
            remote(1, c).start()

        @pl.when((step >= LAG) & (step < n + LAG))
        def _():
            c = step - LAG
            slot = lax.rem(c, slots)
            _, second = partners(c)
            remote(0, c).wait_recv()
            send2[c] = (part[slot, second] + recv1[c, 0].astype(F32)).astype(BF16)
            remote(2, c).start()

        @pl.when((step >= 2 * LAG) & (step < n + 2 * LAG))
        def _():
            c = step - 2 * LAG
            slot = lax.rem(c, slots)
            remote(1, c).wait_recv()
            remote(2, c).wait_recv()
            sums = [
                part[slot, me, k] + recv1[c, 1, k].astype(F32) + recv2[c, k].astype(F32)
                for k in range(3)
            ]
            hidden, d_gate, d_up = activations(*sums)
            acts[c, me, 0] = d_gate
            acts[c, me, 1] = d_up
            remote(3, c).start()
            remote(4, c).start()
            hid[c, me] = hidden

        @pl.when((step >= 3 * LAG) & (step < n + 3 * LAG))
        def _():
            c = step - 3 * LAG
            remote(3, c).wait_recv()
            remote(5, c).start()

        @pl.when(step >= 4 * LAG)
        def _():
            c = step - 4 * LAG
            remote(4, c).wait_recv()
            remote(5, c).wait_recv()
            for copy in results(c):
                copy.start()
            pair = jnp.concatenate(
                [acts[c, :, 0].reshape(-1, chunk), acts[c, :, 1].reshape(-1, chunk)], axis=1
            )
            total[...] += dot_dims(pair, w_pair[c], 1, 1)
            for stage in range(6):
                remote(stage, c).wait_send()

        @pl.when(step == LAG)
        def _():
            scale = 1.0 / math.sqrt(HB)
            for b in range(x_ref.shape[1] // HB):
                columns = pl.ds(b * HB, HB)
                xt_out[columns, :] = (dot_dims(sign_ref[...], x_ref[:, columns], 1, 1) * scale).astype(BF16)
                dyt_out[:, columns] = (dot_dims(dy_ref[:, columns], sign_ref[...], 1, 0) * scale).astype(BF16)

        @pl.when(step == n + LAG)
        def _():
            hidden_copy(0).start()
            hidden_copy(3).start()

    for k in (1, 2):
        hidden_copy(k).start()

    def half(core):
        return pl.ds(pl.multiple_of(core * feats, feats), feats)

    fold = send(total.at[:, half(1 - h)], e1recv, es_sem.at[0], er_sem.at[0], me, sibling)
    fold.start()
    fold.wait()
    for t in range(4):
        block = pl.ds(t * rows, rows)
        e1recv[block, :] = e1recv[block, :] + total[block, half(h)]
        e2send[t] = e1recv[block, :].astype(BF16)

    def piece(k):
        t = (z + k) % 4
        return send(e2send.at[t], e2recv.at[z], es_sem.at[k], er_sem.at[1 + z], me, 2 * t + h)

    for k in (2, 1, 3):
        piece(k).start()
    hidden_copy(0).wait_recv()
    hidden_copy(4).start()
    hidden_copy(1).wait_recv()
    hidden_copy(5).start()
    for k in (1, 3, 2):
        source = (z + k) % 4
        arrived(e2recv.at[source], er_sem.at[1 + source])
    mine = e1recv[span(z, rows), :]
    for k in range(1, 4):
        mine = mine + e2recv[(z + k) % 4].astype(F32)
    e3send[...] = mine.astype(BF16)
    swap = send(e3send, e3recv, es_sem.at[4], er_sem.at[5], z, 2 * me + h)

    @pl.when(me != z)
    def _():
        swap.start()
        swap.wait()
        gt_out[...] = e3recv[...]

    @pl.when(me == z)
    def _():
        gt_out[...] = e3send[...]

    for k in range(2, 6):
        hidden_copy(k).wait_recv()

    @pl.loop(0, n)
    def _(c):
        hidden_result(c).start()

    for k in range(6):
        hidden_copy(k).wait_send()
    for k in range(1, 4):
        piece(k).wait_send()
    for kind in range(2):
        for block in range(4):
            @pl.when((z >= block) & (z < 3))
            def _(block=block, kind=kind):
                upward(block, kind).wait_send()

            @pl.when((z <= block) & (z > 0))
            def _(block=block, kind=kind):
                downward(block, kind).wait_send()

            @pl.when(block != me)
            def _(block=block, kind=kind):
                to_owner(block, kind).wait_send()

            to_core(block, kind).wait_send()

    @pl.loop(0, n)
    def _(c):
        for copy in results(c):
            copy.wait()
        hidden_result(c).wait()


def fused(tokens, grad_out, w_gate, w_up, w_down):
    rows, feats = tokens.shape
    width, units = w_gate.shape
    chunk = 128
    n, count = units // chunk, 4 * rows
    signs = (hadamard(HB) * math.sqrt(HB)).astype(BF16)
    whole, anywhere = pl.BlockSpec(memory_space=pltpu.VMEM), pl.BlockSpec(memory_space=pl.ANY)
    wide = jax.ShapeDtypeStruct((4, rows, units), BF16)
    turned = [jax.ShapeDtypeStruct(dims, BF16) for dims in ((width, count), (count, width))]
    dma = pltpu.SemaphoreType.DMA
    hidden, d_gate, d_up, grad_tokens, x_turned, dy_turned = pl.pallas_call(
        functools.partial(fused_kernel, n),
        out_shape=(wide, wide, wide, jax.ShapeDtypeStruct((rows, feats), BF16), *turned),
        in_specs=[whole] * 3 + [anywhere] * 3,
        out_specs=(anywhere,) * 3 + (whole,) * 3,
        scratch_shapes=[
            pltpu.VMEM((n, width, 2 * chunk), BF16),
            pltpu.VMEM((n, chunk, width), BF16),
            pltpu.VMEM((2 * LAG + 1, 4, 3, rows, chunk), F32),
            pltpu.VMEM((n, 2, 3, rows, chunk), BF16),
            pltpu.VMEM((n, 2, 3, rows, chunk), BF16),
            pltpu.VMEM((n, 3, rows, chunk), BF16),
            pltpu.VMEM((n, 3, rows, chunk), BF16),
            pltpu.VMEM((n, 4, 2, rows, chunk), BF16),
            pltpu.VMEM((n, 4, rows, chunk), BF16),
            pltpu.VMEM((4, 2, rows, feats), BF16),
            pltpu.VMEM((4, 2, 2, rows, feats), BF16),
            pltpu.VMEM((count, width), BF16),
            pltpu.VMEM((count, width), BF16),
            pltpu.VMEM((count, width), F32),
            pltpu.VMEM((count, feats), F32),
            pltpu.VMEM((4, rows, feats), BF16),
            pltpu.VMEM((4, rows, feats), BF16),
            pltpu.VMEM((rows, feats), BF16),
            pltpu.VMEM((rows, feats), BF16),
            dma((3, n)), dma((3, n)), dma((6, n)), dma((6, n)),
            dma((4, 2, 4)), dma((3, 2, 4)), dma((6,)), dma((6,)), dma((5,)), dma((6,)),
        ],
        compiler_params=pltpu.CompilerParams(
            collective_id=0, has_side_effects=True, vmem_limit_bytes=62 * 2**20
        ),
        cost_estimate=pl.CostEstimate(
            flops=10 * count * width * units, bytes_accessed=12 * width * units, transcendentals=0
        ),
    )(tokens, grad_out, signs, w_gate, w_up, w_down)
    flat = [v.reshape(count, units) for v in (hidden, d_gate, d_up)]
    return (grad_tokens, *gradients(x_turned, dy_turned, *flat))


def gradients_kernel(x_ref, dy_ref, hid_ref, dg_ref, du_ref, gate_ref, up_ref, down_ref):
    gate_ref[...] = jnp.dot(x_ref[...], dg_ref[...], preferred_element_type=F32).astype(BF16)
    up_ref[...] = jnp.dot(x_ref[...], du_ref[...], preferred_element_type=F32).astype(BF16)
    down_ref[...] = dot_dims(hid_ref[...], dy_ref[...], 0, 0).astype(BF16)


def gradients(x_turned, dy_turned, hidden, d_gate, d_up):
    width, count = x_turned.shape
    units = hidden.shape[1]
    tile = 512
    once = [pl.BlockSpec(dims, lambda i: (0, 0)) for dims in ((width, count), (count, width))]
    act = pl.BlockSpec((count, tile), lambda i: (0, i))
    grad = pl.BlockSpec((width, tile), lambda i: (0, i))
    wide = jax.ShapeDtypeStruct((width, units), BF16)
    return pl.pallas_call(
        gradients_kernel,
        grid=(units // tile,),
        out_shape=(wide, wide, jax.ShapeDtypeStruct((units, width), BF16)),
        in_specs=[*once, act, act, act],
        out_specs=(grad, grad, pl.BlockSpec((tile, width), lambda i: (i, 0))),
        compiler_params=pltpu.CompilerParams(vmem_limit_bytes=48 * 2**20),
        cost_estimate=pl.CostEstimate(
            flops=6 * count * width * units, bytes_accessed=12 * width * units, transcendentals=0
        ),
    )(x_turned, dy_turned, hidden, d_gate, d_up)


def plain(n_rep, n_fsdp, tokens, grad_out, w_gate, w_up, w_down):
    x_block, dy_block = gather_blocks(tokens, grad_out)
    hidden, d_gate, d_up, partial = middle_plain(x_block, dy_block, w_gate, w_up, w_down)
    grad_tokens = scatter_tokens(partial, n_rep, n_fsdp)
    x_turned, dy_turned = rotate_features(x_block), rotate_features(dy_block)
    return (
        grad_tokens,
        dot_dims(x_turned, d_gate, 0, 0).astype(BF16),
        dot_dims(x_turned, d_up, 0, 0).astype(BF16),
        dot_dims(hidden, dy_turned, 0, 0).astype(BF16),
    )


def solution(mesh):
    n_rep, n_fsdp = mesh.shape["rep"], mesh.shape["fsdp"]
    body = fused if (n_rep, n_fsdp) == (8, 4) else functools.partial(plain, n_rep, n_fsdp)
    return jax.shard_map(
        body,
        mesh=mesh,
        in_specs=(P("fsdp", "rep"),) * 4 + (P("rep", "fsdp"),),
        out_specs=(P("fsdp", "rep"),) * 3 + (P("rep", "fsdp"),),
        check_vma=False,
    )
```

```python
import functools
import math

import jax
import jax.numpy as jnp
from jax import lax
from jax.experimental import pallas as pl
from jax.experimental.pallas import tpu as pltpu
from jax.sharding import PartitionSpec as P

HB = 128
BF16 = jnp.bfloat16
F32 = jnp.float32


def hadamard(size):
    index = jnp.arange(size, dtype=jnp.int32)
    both = index[:, None] & index[None, :]
    parity = jnp.zeros((size, size), jnp.int32)
    for bit_pos in range(size.bit_length() - 1):
        parity = parity + (both >> bit_pos & 1)
    return (1 - 2 * (parity % 2)).astype(F32) / math.sqrt(size)


def dot_dims(left, right, left_dim, right_dim, kind=F32):
    return lax.dot_general(
        left, right, (((left_dim,), (right_dim,)), ((), ())), preferred_element_type=kind
    )


def rotate_features(block):
    rows, width = block.shape
    parts = block.astype(F32).reshape(rows, width // HB, HB)
    turned = jnp.einsum("tbj,ij->tbi", parts, hadamard(HB), precision=lax.Precision.HIGHEST)
    return turned.reshape(rows, width).astype(BF16)


def gather_blocks(tokens, grad_out):
    both = jnp.stack([tokens, grad_out])
    full = lax.all_gather(both, "rep", axis=2, tiled=True)
    block = lax.all_to_all(full, "fsdp", split_axis=2, concat_axis=1, tiled=True)
    return block[0], block[1]


def activations(gate, up, d_hidden):
    sig = jax.nn.sigmoid(gate)
    active = gate * sig
    hidden = (active * up).astype(BF16)
    d_gate = (d_hidden * up * sig * (1.0 + gate * (1.0 - sig))).astype(BF16)
    d_up = (d_hidden * active).astype(BF16)
    return hidden, d_gate, d_up


def middle_plain(x_block, dy_block, w_gate, w_up, w_down):
    sums = [
        lax.psum_scatter(part, "fsdp", scatter_dimension=0, tiled=True)
        for part in (
            dot_dims(x_block, w_gate, 1, 0),
            dot_dims(x_block, w_up, 1, 0),
            dot_dims(dy_block, w_down, 1, 1),
        )
    ]
    own = activations(*sums)
    hidden, d_gate, d_up = [lax.all_gather(v, "fsdp", axis=0, tiled=True) for v in own]
    partial = dot_dims(d_gate, w_gate, 1, 1) + dot_dims(d_up, w_up, 1, 1)
    return hidden, d_gate, d_up, partial


def scatter_tokens(partial, n_rep, n_fsdp):
    rows, width = partial.shape
    halves = n_rep // n_fsdp
    pieces = partial.reshape(n_fsdp, rows // n_fsdp, halves, width // halves)
    pieces = pieces.transpose(0, 2, 1, 3).reshape(n_rep, rows // n_fsdp, width // halves)
    piece = lax.psum_scatter(pieces, "rep", scatter_dimension=0, tiled=False)
    pairs = []
    for f in range(n_fsdp):
        for r in range(n_rep):
            t, h = divmod(r, halves)
            pairs.append((r * n_fsdp + f, (f * halves + h) * n_fsdp + t))
    return lax.ppermute(piece.astype(BF16), ("rep", "fsdp"), pairs)


MESH = pl.DeviceIdType.MESH
LAG = 3
EARLY = 4


def fused_kernel(
    n, tok_ref, go_ref, sign_ref, wg_hbm, wu_hbm, wd_hbm,
    hid_out, dg_out, du_out, gt_out, xt_out, dyt_out,
    w_pair, w_low, part, send1, recv1, send2, recv2, acts, hid,
    zbuf, gath, x_ref, dy_ref, total, e1recv, e2send, e2recv, e3send, e3recv,
    w_sem, out_sem, ssem, rsem, gs_sem, gr_sem, hs_sem, hr_sem, es_sem, er_sem,
):
    chunk = w_low.shape[1]
    slots = part.shape[0]
    rows, feats = tok_ref.shape
    me, rep = lax.axis_index("fsdp"), lax.axis_index("rep")
    z, h = rep // 2, rep % 2
    sibling = rep + 1 - 2 * h
    y, x = me // 2, me % 2
    near_x, near_y, far = 2 * y + 1 - x, 2 * (1 - y) + x, 3 - me

    def span(c, size):
        return pl.ds(pl.multiple_of(c * size, size), size)

    def send(source, target, send_sem, recv_sem, fsdp, to):
        return pltpu.make_async_remote_copy(
            src_ref=source, dst_ref=target, send_sem=send_sem, recv_sem=recv_sem,
            device_id={"rep": to, "fsdp": fsdp}, device_id_type=MESH,
        )

    def weight(k, c):
        columns = span(c, chunk)
        source, target = (
            (wg_hbm.at[:, columns], w_pair.at[c, :, pl.ds(0, chunk)]),
            (wu_hbm.at[:, columns], w_pair.at[c, :, pl.ds(chunk, chunk)]),
            (wd_hbm.at[columns, :], w_low.at[c]),
        )[k]
        return pltpu.make_async_copy(source, target, w_sem.at[k, c])

    def results(c):
        return [
            pltpu.make_async_copy(acts.at[c, :, k], out.at[:, :, span(c, chunk)], out_sem.at[k, c])
            for k, out in enumerate((dg_out, du_out))
        ]

    def hidden_result(c):
        return pltpu.make_async_copy(hid.at[c], hid_out.at[:, :, span(c, chunk)], out_sem.at[2, c])

    def partners(c):
        odd = lax.rem(c, 2)
        first = near_x * (1 - odd) + near_y * odd
        return first, near_x + near_y - first

    def remote(stage, c):
        first, second = partners(c)
        source, target, device = (
            (send1.at[c, 0, pl.ds(0, 2)], recv1.at[c, 0, pl.ds(0, 2)], first),
            (send1.at[c, 1, pl.ds(0, 2)], recv1.at[c, 1, pl.ds(0, 2)], first),
            (send2.at[c], recv2.at[c], second),
            (acts.at[c, me], acts.at[c, me], first),
            (acts.at[c, me], acts.at[c, me], second),
            (acts.at[c, first], acts.at[c, first], second),
            (send1.at[c, 0, 2], recv1.at[c, 0, 2], first),
            (send1.at[c, 1, 2], recv1.at[c, 1, 2], first),
        )[stage]
        return send(source, target, ssem.at[stage, c], rsem.at[stage, c], device, rep)

    @pl.loop(0, n)
    def _(c):
        for k in range(3):
            weight(k, c).start()

    zbuf[z, 0] = tok_ref[...]
    zbuf[z, 1] = go_ref[...]

    barrier = pltpu.get_barrier_semaphore()

    def greet(fsdp, to):
        pl.semaphore_signal(
            barrier, inc=1, device_id={"rep": to, "fsdp": fsdp}, device_id_type=MESH
        )

    for k in range(1, 4):
        greet(me, 2 * ((z + k) % 4) + h)
        greet((me + k) % 4, rep)
    greet(me, sibling)

    @pl.when(me != z)
    def _():
        greet(z, 2 * me + h)

    pl.semaphore_wait(barrier, 7 + jnp.where(me != z, 1, 0))

    total[...] = jnp.zeros_like(total)

    def upward(block, kind):
        here = zbuf.at[block, kind]
        return send(here, here, gs_sem.at[0, kind, block], gr_sem.at[0, kind, block], me, rep + 2)

    def downward(block, kind):
        here = zbuf.at[block, kind]
        return send(here, here, gs_sem.at[1, kind, block], gr_sem.at[0, kind, block], me, rep - 2)

    def to_owner(block, kind):
        return send(
            zbuf.at[block, kind], gath.at[me, h, kind],
            gs_sem.at[2, kind, block], gr_sem.at[1, kind, me], block, rep,
        )

    def to_core(owner, kind):
        here = gath.at[owner, h, kind]
        return send(here, here, gs_sem.at[3, kind, owner], gr_sem.at[2, kind, owner], me, sibling)

    def arrived(target, sem):
        pltpu.make_async_copy(target, target, sem).wait()

    def pass_on(block, kind):
        @pl.when(block != me)
        def _():
            to_owner(block, kind).start()

        @pl.when(block == me)
        def _():
            gath[me, h, kind] = zbuf[block, kind]
            to_core(me, kind).start()

    def relay(block, kind, go, copy):
        @pl.when(go)
        def _():
            copy(block, kind).start()

    def own(kind):
        relay(z, kind, z < 3, upward)
        relay(z, kind, z > 0, downward)
        pass_on(z, kind)

    def from_afar(k, kind):
        for block, there, go, copy in (
            (z - k, z >= k, z < 3, upward), (z + k, z + k < 4, z > 0, downward),
        ):
            @pl.when(there)
            def _(block=block, go=go, copy=copy):
                arrived(zbuf.at[block, kind], gr_sem.at[0, kind, block])
                relay(block, kind, go, copy)
                pass_on(block, kind)

    def hand_over(kind):
        for k in range(1, 4):
            owner = (me + k) % 4
            arrived(gath.at[owner, h, kind], gr_sem.at[1, kind, owner])
            to_core(owner, kind).start()

    def assemble(kind, target):
        for k in range(4):
            owner = (me + k) % 4
            arrived(gath.at[owner, 1 - h, kind], gr_sem.at[2, kind, owner])
        for owner in range(4):
            for side in range(2):
                place = (pl.ds(owner * rows, rows), pl.ds(side * feats, feats))
                target[place] = gath[owner, side, kind]

    def start_pair(c):
        slot = lax.rem(c, slots)
        first, _ = partners(c)
        for k in range(2):
            weight(k, c).wait()
        pair = jnp.dot(x_ref[...], w_pair[c], preferred_element_type=F32)
        part[slot, :, 0] = pair[:, :chunk].reshape(4, -1, chunk)
        part[slot, :, 1] = pair[:, chunk:].reshape(4, -1, chunk)
        for stage, block in enumerate((far, first)):
            for k in range(2):
                send1[c, stage, k] = part[slot, block, k].astype(BF16)
            remote(stage, c).start()

    def start_low(c):
        slot = lax.rem(c, slots)
        first, _ = partners(c)
        weight(2, c).wait()
        part[slot, :, 2] = dot_dims(dy_ref[...], w_low[c], 1, 1).reshape(4, -1, chunk)
        for stage, block in enumerate((far, first)):
            send1[c, stage, 2] = part[slot, block, 2].astype(BF16)
            remote(6 + stage, c).start()

    own(0)
    from_afar(1, 0)
    own(1)
    from_afar(2, 0)
    from_afar(1, 1)
    from_afar(3, 0)
    from_afar(2, 1)
    hand_over(0)
    assemble(0, x_ref)
    pl.loop(0, EARLY // 2)(start_pair)
    from_afar(3, 1)
    hand_over(1)
    pl.loop(EARLY // 2, EARLY)(start_pair)
    assemble(1, dy_ref)

    low, high = pl.ds(0, n // 2), pl.ds(n // 2, n - n // 2)

    def hidden_copy(k):
        part_of, owner, device = (
            (low, me, near_x), (high, me, near_y), (high, me, near_x), (low, me, near_y),
            (low, near_x, near_y), (high, near_y, near_x),
        )[k]
        block = hid.at[part_of, owner]
        return send(block, block, hs_sem.at[k], hr_sem.at[k], device, rep)

    @pl.loop(0, n + 4 * LAG)
    def _(step):
        @pl.when(step < n)
        def _():
            @pl.when(step >= EARLY)
            def _():
                start_pair(step)

            start_low(step)

        @pl.when((step >= LAG) & (step < n + LAG))
        def _():
            c = step - LAG
            slot = lax.rem(c, slots)
            _, second = partners(c)
            remote(0, c).wait_recv()
            remote(6, c).wait_recv()
            send2[c] = (part[slot, second] + recv1[c, 0].astype(F32)).astype(BF16)
            remote(2, c).start()

        @pl.when((step >= 2 * LAG) & (step < n + 2 * LAG))
        def _():
            c = step - 2 * LAG
            slot = lax.rem(c, slots)
            remote(1, c).wait_recv()
            remote(7, c).wait_recv()
            remote(2, c).wait_recv()
            sums = [
                part[slot, me, k] + recv1[c, 1, k].astype(F32) + recv2[c, k].astype(F32)
                for k in range(3)
            ]
            hidden, d_gate, d_up = activations(*sums)
            acts[c, me, 0] = d_gate
            acts[c, me, 1] = d_up
            remote(3, c).start()
            remote(4, c).start()
            hid[c, me] = hidden

        @pl.when((step >= 3 * LAG) & (step < n + 3 * LAG))
        def _():
            c = step - 3 * LAG
            remote(3, c).wait_recv()
            remote(5, c).start()

        @pl.when(step >= 4 * LAG)
        def _():
            c = step - 4 * LAG
            remote(4, c).wait_recv()
            remote(5, c).wait_recv()
            for copy in results(c):
                copy.start()
            pair = jnp.concatenate(
                [acts[c, :, 0].reshape(-1, chunk), acts[c, :, 1].reshape(-1, chunk)], axis=1
            )
            total[...] += dot_dims(pair, w_pair[c], 1, 1)
            for stage in range(8):
                remote(stage, c).wait_send()

        @pl.when(step == LAG)
        def _():
            scale = 1.0 / math.sqrt(HB)
            for b in range(x_ref.shape[1] // HB):
                columns = pl.ds(b * HB, HB)
                xt_out[columns, :] = (dot_dims(sign_ref[...], x_ref[:, columns], 1, 1) * scale).astype(BF16)
                dyt_out[:, columns] = (dot_dims(dy_ref[:, columns], sign_ref[...], 1, 0) * scale).astype(BF16)

        @pl.when(step == n + LAG)
        def _():
            hidden_copy(0).start()
            hidden_copy(3).start()

    for k in (1, 2):
        hidden_copy(k).start()

    def half(core):
        return pl.ds(pl.multiple_of(core * feats, feats), feats)

    fold = send(total.at[:, half(1 - h)], e1recv, es_sem.at[0], er_sem.at[0], me, sibling)
    fold.start()
    fold.wait()
    for t in range(4):
        block = pl.ds(t * rows, rows)
        e1recv[block, :] = e1recv[block, :] + total[block, half(h)]
        e2send[t] = e1recv[block, :].astype(BF16)

    def piece(k):
        t = (z + k) % 4
        return send(e2send.at[t], e2recv.at[z], es_sem.at[k], er_sem.at[1 + z], me, 2 * t + h)

    for k in (2, 1, 3):
        piece(k).start()
    hidden_copy(0).wait_recv()
    hidden_copy(4).start()
    hidden_copy(1).wait_recv()
    hidden_copy(5).start()
    for k in (1, 3, 2):
        source = (z + k) % 4
        arrived(e2recv.at[source], er_sem.at[1 + source])
    mine = e1recv[span(z, rows), :]
    for k in range(1, 4):
        mine = mine + e2recv[(z + k) % 4].astype(F32)
    e3send[...] = mine.astype(BF16)
    swap = send(e3send, e3recv, es_sem.at[4], er_sem.at[5], z, 2 * me + h)

    @pl.when(me != z)
    def _():
        swap.start()
        swap.wait()
        gt_out[...] = e3recv[...]

    @pl.when(me == z)
    def _():
        gt_out[...] = e3send[...]

    for k in range(2, 6):
        hidden_copy(k).wait_recv()

    @pl.loop(0, n)
    def _(c):
        hidden_result(c).start()

    for k in range(6):
        hidden_copy(k).wait_send()
    for k in range(1, 4):
        piece(k).wait_send()
    for kind in range(2):
        for block in range(4):
            @pl.when((z >= block) & (z < 3))
            def _(block=block, kind=kind):
                upward(block, kind).wait_send()

            @pl.when((z <= block) & (z > 0))
            def _(block=block, kind=kind):
                downward(block, kind).wait_send()

            @pl.when(block != me)
            def _(block=block, kind=kind):
                to_owner(block, kind).wait_send()

            to_core(block, kind).wait_send()

    @pl.loop(0, n)
    def _(c):
        for copy in results(c):
            copy.wait()
        hidden_result(c).wait()


def fused(tokens, grad_out, w_gate, w_up, w_down):
    rows, feats = tokens.shape
    width, units = w_gate.shape
    chunk = 128
    n, count = units // chunk, 4 * rows
    signs = (hadamard(HB) * math.sqrt(HB)).astype(BF16)
    whole, anywhere = pl.BlockSpec(memory_space=pltpu.VMEM), pl.BlockSpec(memory_space=pl.ANY)
    wide = jax.ShapeDtypeStruct((4, rows, units), BF16)
    turned = [jax.ShapeDtypeStruct(dims, BF16) for dims in ((width, count), (count, width))]
    dma = pltpu.SemaphoreType.DMA
    hidden, d_gate, d_up, grad_tokens, x_turned, dy_turned = pl.pallas_call(
        functools.partial(fused_kernel, n),
        out_shape=(wide, wide, wide, jax.ShapeDtypeStruct((rows, feats), BF16), *turned),
        in_specs=[whole] * 3 + [anywhere] * 3,
        out_specs=(anywhere,) * 3 + (whole,) * 3,
        scratch_shapes=[
            pltpu.VMEM((n, width, 2 * chunk), BF16),
            pltpu.VMEM((n, chunk, width), BF16),
            pltpu.VMEM((2 * LAG + 1, 4, 3, rows, chunk), F32),
            pltpu.VMEM((n, 2, 3, rows, chunk), BF16),
            pltpu.VMEM((n, 2, 3, rows, chunk), BF16),
            pltpu.VMEM((n, 3, rows, chunk), BF16),
            pltpu.VMEM((n, 3, rows, chunk), BF16),
            pltpu.VMEM((n, 4, 2, rows, chunk), BF16),
            pltpu.VMEM((n, 4, rows, chunk), BF16),
            pltpu.VMEM((4, 2, rows, feats), BF16),
            pltpu.VMEM((4, 2, 2, rows, feats), BF16),
            pltpu.VMEM((count, width), BF16),
            pltpu.VMEM((count, width), BF16),
            pltpu.VMEM((count, width), F32),
            pltpu.VMEM((count, feats), F32),
            pltpu.VMEM((4, rows, feats), BF16),
            pltpu.VMEM((4, rows, feats), BF16),
            pltpu.VMEM((rows, feats), BF16),
            pltpu.VMEM((rows, feats), BF16),
            dma((3, n)), dma((3, n)), dma((8, n)), dma((8, n)),
            dma((4, 2, 4)), dma((3, 2, 4)), dma((6,)), dma((6,)), dma((5,)), dma((6,)),
        ],
        compiler_params=pltpu.CompilerParams(
            collective_id=0, has_side_effects=True, vmem_limit_bytes=62 * 2**20
        ),
        cost_estimate=pl.CostEstimate(
            flops=10 * count * width * units, bytes_accessed=12 * width * units, transcendentals=0
        ),
    )(tokens, grad_out, signs, w_gate, w_up, w_down)
    flat = [v.reshape(count, units) for v in (hidden, d_gate, d_up)]
    return (grad_tokens, *gradients(x_turned, dy_turned, *flat))


def gradients_kernel(x_ref, dy_ref, hid_ref, dg_ref, du_ref, gate_ref, up_ref, down_ref):
    gate_ref[...] = jnp.dot(x_ref[...], dg_ref[...], preferred_element_type=F32).astype(BF16)
    up_ref[...] = jnp.dot(x_ref[...], du_ref[...], preferred_element_type=F32).astype(BF16)
    down_ref[...] = dot_dims(hid_ref[...], dy_ref[...], 0, 0).astype(BF16)


def gradients(x_turned, dy_turned, hidden, d_gate, d_up):
    width, count = x_turned.shape
    units = hidden.shape[1]
    tile = 256
    once = [pl.BlockSpec(dims, lambda i: (0, 0)) for dims in ((width, count), (count, width))]
    act = pl.BlockSpec((count, tile), lambda i: (0, i))
    grad = pl.BlockSpec((width, tile), lambda i: (0, i))
    wide = jax.ShapeDtypeStruct((width, units), BF16)
    return pl.pallas_call(
        gradients_kernel,
        grid=(units // tile,),
        out_shape=(wide, wide, jax.ShapeDtypeStruct((units, width), BF16)),
        in_specs=[*once, act, act, act],
        out_specs=(grad, grad, pl.BlockSpec((tile, width), lambda i: (i, 0))),
        compiler_params=pltpu.CompilerParams(vmem_limit_bytes=60 * 2**20),
        cost_estimate=pl.CostEstimate(
            flops=6 * count * width * units, bytes_accessed=12 * width * units, transcendentals=0
        ),
    )(x_turned, dy_turned, hidden, d_gate, d_up)


def plain(n_rep, n_fsdp, tokens, grad_out, w_gate, w_up, w_down):
    x_block, dy_block = gather_blocks(tokens, grad_out)
    hidden, d_gate, d_up, partial = middle_plain(x_block, dy_block, w_gate, w_up, w_down)
    grad_tokens = scatter_tokens(partial, n_rep, n_fsdp)
    x_turned, dy_turned = rotate_features(x_block), rotate_features(dy_block)
    return (
        grad_tokens,
        dot_dims(x_turned, d_gate, 0, 0).astype(BF16),
        dot_dims(x_turned, d_up, 0, 0).astype(BF16),
        dot_dims(hidden, dy_turned, 0, 0).astype(BF16),
    )


def solution(mesh):
    n_rep, n_fsdp = mesh.shape["rep"], mesh.shape["fsdp"]
    body = fused if (n_rep, n_fsdp) == (8, 4) else functools.partial(plain, n_rep, n_fsdp)
    return jax.shard_map(
        body,
        mesh=mesh,
        in_specs=(P("fsdp", "rep"),) * 4 + (P("rep", "fsdp"),),
        out_specs=(P("fsdp", "rep"),) * 3 + (P("rep", "fsdp"),),
        check_vma=False,
    )
```

```python
import functools
import math

import jax
import jax.numpy as jnp
from jax import lax
from jax.experimental import pallas as pl
from jax.experimental.pallas import tpu as pltpu
from jax.sharding import PartitionSpec as P

HB = 128
BF16 = jnp.bfloat16
F32 = jnp.float32


def hadamard(size):
    index = jnp.arange(size, dtype=jnp.int32)
    both = index[:, None] & index[None, :]
    parity = jnp.zeros((size, size), jnp.int32)
    for bit_pos in range(size.bit_length() - 1):
        parity = parity + (both >> bit_pos & 1)
    return (1 - 2 * (parity % 2)).astype(F32) / math.sqrt(size)


def dot_dims(left, right, left_dim, right_dim, kind=F32):
    return lax.dot_general(
        left, right, (((left_dim,), (right_dim,)), ((), ())), preferred_element_type=kind
    )


def rotate_features(block):
    rows, width = block.shape
    parts = block.astype(F32).reshape(rows, width // HB, HB)
    turned = jnp.einsum("tbj,ij->tbi", parts, hadamard(HB), precision=lax.Precision.HIGHEST)
    return turned.reshape(rows, width).astype(BF16)


def gather_blocks(tokens, grad_out):
    both = jnp.stack([tokens, grad_out])
    full = lax.all_gather(both, "rep", axis=2, tiled=True)
    block = lax.all_to_all(full, "fsdp", split_axis=2, concat_axis=1, tiled=True)
    return block[0], block[1]


def activations(gate, up, d_hidden):
    sig = jax.nn.sigmoid(gate)
    active = gate * sig
    hidden = (active * up).astype(BF16)
    d_gate = (d_hidden * up * sig * (1.0 + gate * (1.0 - sig))).astype(BF16)
    d_up = (d_hidden * active).astype(BF16)
    return hidden, d_gate, d_up


def middle_plain(x_block, dy_block, w_gate, w_up, w_down):
    sums = [
        lax.psum_scatter(part, "fsdp", scatter_dimension=0, tiled=True)
        for part in (
            dot_dims(x_block, w_gate, 1, 0),
            dot_dims(x_block, w_up, 1, 0),
            dot_dims(dy_block, w_down, 1, 1),
        )
    ]
    own = activations(*sums)
    hidden, d_gate, d_up = [lax.all_gather(v, "fsdp", axis=0, tiled=True) for v in own]
    partial = dot_dims(d_gate, w_gate, 1, 1) + dot_dims(d_up, w_up, 1, 1)
    return hidden, d_gate, d_up, partial


def scatter_tokens(partial, n_rep, n_fsdp):
    rows, width = partial.shape
    halves = n_rep // n_fsdp
    pieces = partial.reshape(n_fsdp, rows // n_fsdp, halves, width // halves)
    pieces = pieces.transpose(0, 2, 1, 3).reshape(n_rep, rows // n_fsdp, width // halves)
    piece = lax.psum_scatter(pieces, "rep", scatter_dimension=0, tiled=False)
    pairs = []
    for f in range(n_fsdp):
        for r in range(n_rep):
            t, h = divmod(r, halves)
            pairs.append((r * n_fsdp + f, (f * halves + h) * n_fsdp + t))
    return lax.ppermute(piece.astype(BF16), ("rep", "fsdp"), pairs)


MESH = pl.DeviceIdType.MESH
LAG = 3
EARLY = 4


def fused_kernel(
    n, tok_ref, go_ref, sign_ref, wg_hbm, wu_hbm, wd_hbm,
    hid_out, dg_out, du_out, gt_out, xt_out, dyt_out,
    w_pair, w_low, part, send1, recv1, send2, recv2, acts, hid,
    zbuf, gath, x_ref, dy_ref, total, e1recv, e2send, e2recv, e3send, e3recv,
    w_sem, out_sem, ssem, rsem, gs_sem, gr_sem, hs_sem, hr_sem, es_sem, er_sem,
):
    chunk = w_low.shape[1]
    slots = part.shape[0]
    rows, feats = tok_ref.shape
    me, rep = lax.axis_index("fsdp"), lax.axis_index("rep")
    z, h = rep // 2, rep % 2
    sibling = rep + 1 - 2 * h
    y, x = me // 2, me % 2
    near_x, near_y, far = 2 * y + 1 - x, 2 * (1 - y) + x, 3 - me

    def span(c, size):
        return pl.ds(pl.multiple_of(c * size, size), size)

    def send(source, target, send_sem, recv_sem, fsdp, to):
        return pltpu.make_async_remote_copy(
            src_ref=source, dst_ref=target, send_sem=send_sem, recv_sem=recv_sem,
            device_id={"rep": to, "fsdp": fsdp}, device_id_type=MESH,
        )

    def weight(k, c):
        columns = span(c, chunk)
        source, target = (
            (wg_hbm.at[:, columns], w_pair.at[c, :, pl.ds(0, chunk)]),
            (wu_hbm.at[:, columns], w_pair.at[c, :, pl.ds(chunk, chunk)]),
            (wd_hbm.at[columns, :], w_low.at[c]),
        )[k]
        return pltpu.make_async_copy(source, target, w_sem.at[k, c])

    def results(c):
        return [
            pltpu.make_async_copy(acts.at[c, :, k], out.at[:, :, span(c, chunk)], out_sem.at[k, c])
            for k, out in enumerate((dg_out, du_out))
        ]

    def hidden_result(c):
        return pltpu.make_async_copy(hid.at[c], hid_out.at[:, :, span(c, chunk)], out_sem.at[2, c])

    def partners(c):
        odd = lax.rem(c, 2)
        first = near_x * (1 - odd) + near_y * odd
        return first, near_x + near_y - first

    def remote(stage, c):
        first, second = partners(c)
        source, target, device = (
            (send1.at[c, 0, pl.ds(0, 2)], recv1.at[c, 0, pl.ds(0, 2)], first),
            (send1.at[c, 1, pl.ds(0, 2)], recv1.at[c, 1, pl.ds(0, 2)], first),
            (send2.at[c], recv2.at[c], second),
            (acts.at[c, me], acts.at[c, me], first),
            (acts.at[c, me], acts.at[c, me], second),
            (acts.at[c, first], acts.at[c, first], second),
            (send1.at[c, 0, 2], recv1.at[c, 0, 2], first),
            (send1.at[c, 1, 2], recv1.at[c, 1, 2], first),
        )[stage]
        return send(source, target, ssem.at[stage, c], rsem.at[stage, c], device, rep)

    @pl.loop(0, n)
    def _(c):
        for k in range(3):
            weight(k, c).start()

    zbuf[z, 0] = tok_ref[...]
    zbuf[z, 1] = go_ref[...]

    barrier = pltpu.get_barrier_semaphore()

    def greet(fsdp, to):
        pl.semaphore_signal(
            barrier, inc=1, device_id={"rep": to, "fsdp": fsdp}, device_id_type=MESH
        )

    for k in range(1, 4):
        greet(me, 2 * ((z + k) % 4) + h)
        greet((me + k) % 4, rep)
    greet(me, sibling)

    @pl.when(me != z)
    def _():
        greet(z, 2 * me + h)

    pl.semaphore_wait(barrier, 7 + jnp.where(me != z, 1, 0))

    total[...] = jnp.zeros_like(total)

    def upward(block, kind):
        here = zbuf.at[block, kind]
        return send(here, here, gs_sem.at[0, kind, block], gr_sem.at[0, kind, block], me, rep + 2)

    def downward(block, kind):
        here = zbuf.at[block, kind]
        return send(here, here, gs_sem.at[1, kind, block], gr_sem.at[0, kind, block], me, rep - 2)

    def to_owner(block, kind):
        return send(
            zbuf.at[block, kind], gath.at[me, h, kind],
            gs_sem.at[2, kind, block], gr_sem.at[1, kind, me], block, rep,
        )

    def to_core(owner, kind):
        here = gath.at[owner, h, kind]
        return send(here, here, gs_sem.at[3, kind, owner], gr_sem.at[2, kind, owner], me, sibling)

    def arrived(target, sem):
        pltpu.make_async_copy(target, target, sem).wait()

    def pass_on(block, kind):
        @pl.when(block != me)
        def _():
            to_owner(block, kind).start()

        @pl.when(block == me)
        def _():
            gath[me, h, kind] = zbuf[block, kind]
            to_core(me, kind).start()

    def relay(block, kind, go, copy):
        @pl.when(go)
        def _():
            copy(block, kind).start()

    def own(kind):
        relay(z, kind, z < 3, upward)
        relay(z, kind, z > 0, downward)
        pass_on(z, kind)

    def from_afar(k, kind):
        for block, there, go, copy in (
            (z - k, z >= k, z < 3, upward), (z + k, z + k < 4, z > 0, downward),
        ):
            @pl.when(there)
            def _(block=block, go=go, copy=copy):
                arrived(zbuf.at[block, kind], gr_sem.at[0, kind, block])
                relay(block, kind, go, copy)
                pass_on(block, kind)

    def hand_over(kind):
        for k in range(1, 4):
            owner = (me + k) % 4
            arrived(gath.at[owner, h, kind], gr_sem.at[1, kind, owner])
            to_core(owner, kind).start()

    def assemble(kind, target):
        for k in range(4):
            owner = (me + k) % 4
            arrived(gath.at[owner, 1 - h, kind], gr_sem.at[2, kind, owner])
        for owner in range(4):
            for side in range(2):
                place = (pl.ds(owner * rows, rows), pl.ds(side * feats, feats))
                target[place] = gath[owner, side, kind]

    def start_pair(c):
        slot = lax.rem(c, slots)
        first, _ = partners(c)
        for k in range(2):
            weight(k, c).wait()
        pair = jnp.dot(x_ref[...], w_pair[c], preferred_element_type=F32)
        part[slot, :, 0] = pair[:, :chunk].reshape(4, -1, chunk)
        part[slot, :, 1] = pair[:, chunk:].reshape(4, -1, chunk)
        for stage, block in enumerate((far, first)):
            for k in range(2):
                send1[c, stage, k] = part[slot, block, k].astype(BF16)
            remote(stage, c).start()

    def start_low(c):
        slot = lax.rem(c, slots)
        first, _ = partners(c)
        weight(2, c).wait()
        part[slot, :, 2] = dot_dims(dy_ref[...], w_low[c], 1, 1).reshape(4, -1, chunk)
        for stage, block in enumerate((far, first)):
            send1[c, stage, 2] = part[slot, block, 2].astype(BF16)
            remote(6 + stage, c).start()

    own(0)
    from_afar(1, 0)
    own(1)
    from_afar(2, 0)
    from_afar(1, 1)
    from_afar(3, 0)
    from_afar(2, 1)
    hand_over(0)
    assemble(0, x_ref)
    pl.loop(0, EARLY // 2)(start_pair)
    from_afar(3, 1)
    hand_over(1)
    pl.loop(EARLY // 2, EARLY)(start_pair)
    assemble(1, dy_ref)

    low, high = pl.ds(0, n // 2), pl.ds(n // 2, n - n // 2)

    def hidden_copy(k):
        part_of, owner, device = (
            (low, me, near_x), (high, me, near_y), (high, me, near_x), (low, me, near_y),
            (low, near_x, near_y), (high, near_y, near_x),
        )[k]
        block = hid.at[part_of, owner]
        return send(block, block, hs_sem.at[k], hr_sem.at[k], device, rep)

    @pl.loop(0, n + 4 * LAG)
    def _(step):
        @pl.when(step < n)
        def _():
            @pl.when(step >= EARLY)
            def _():
                start_pair(step)

            start_low(step)

        @pl.when((step >= LAG) & (step < n + LAG))
        def _():
            c = step - LAG
            slot = lax.rem(c, slots)
            _, second = partners(c)
            remote(0, c).wait_recv()
            remote(6, c).wait_recv()
            send2[c] = (part[slot, second] + recv1[c, 0].astype(F32)).astype(BF16)
            remote(2, c).start()

        @pl.when((step >= 2 * LAG) & (step < n + 2 * LAG))
        def _():
            c = step - 2 * LAG
            slot = lax.rem(c, slots)
            remote(1, c).wait_recv()
            remote(7, c).wait_recv()
            remote(2, c).wait_recv()
            sums = [
                part[slot, me, k] + recv1[c, 1, k].astype(F32) + recv2[c, k].astype(F32)
                for k in range(3)
            ]
            hidden, d_gate, d_up = activations(*sums)
            acts[c, me, 0] = d_gate
            acts[c, me, 1] = d_up
            remote(3, c).start()
            remote(4, c).start()
            hid[c, me] = hidden

        @pl.when((step >= 3 * LAG) & (step < n + 3 * LAG))
        def _():
            c = step - 3 * LAG
            remote(3, c).wait_recv()
            remote(5, c).start()

        @pl.when(step >= 4 * LAG)
        def _():
            c = step - 4 * LAG
            remote(4, c).wait_recv()
            remote(5, c).wait_recv()
            for copy in results(c):
                copy.start()
            pair = jnp.concatenate(
                [acts[c, :, 0].reshape(-1, chunk), acts[c, :, 1].reshape(-1, chunk)], axis=1
            )
            total[...] += dot_dims(pair, w_pair[c], 1, 1)
            for stage in range(8):
                remote(stage, c).wait_send()

        @pl.when(step == LAG)
        def _():
            scale = 1.0 / math.sqrt(HB)
            for b in range(x_ref.shape[1] // HB):
                columns = pl.ds(b * HB, HB)
                xt_out[columns, :] = (dot_dims(sign_ref[...], x_ref[:, columns], 1, 1) * scale).astype(BF16)
                dyt_out[:, columns] = (dot_dims(dy_ref[:, columns], sign_ref[...], 1, 0) * scale).astype(BF16)

        @pl.when(step == n + LAG)
        def _():
            hidden_copy(0).start()
            hidden_copy(3).start()

    for k in (1, 2):
        hidden_copy(k).start()

    def half(core):
        return pl.ds(pl.multiple_of(core * feats, feats), feats)

    fold = send(total.at[:, half(1 - h)], e1recv, es_sem.at[0], er_sem.at[0], me, sibling)
    fold.start()
    fold.wait()
    for t in range(4):
        block = pl.ds(t * rows, rows)
        e1recv[block, :] = e1recv[block, :] + total[block, half(h)]
        e2send[t] = e1recv[block, :].astype(BF16)

    def piece(k):
        t = (z + k) % 4
        return send(e2send.at[t], e2recv.at[z], es_sem.at[k], er_sem.at[1 + z], me, 2 * t + h)

    for k in (2, 1, 3):
        piece(k).start()
    hidden_copy(0).wait_recv()
    hidden_copy(4).start()
    hidden_copy(1).wait_recv()
    hidden_copy(5).start()
    for k in (1, 3, 2):
        source = (z + k) % 4
        arrived(e2recv.at[source], er_sem.at[1 + source])
    mine = e1recv[span(z, rows), :]
    for k in range(1, 4):
        mine = mine + e2recv[(z + k) % 4].astype(F32)
    e3send[...] = mine.astype(BF16)
    swap = send(e3send, e3recv, es_sem.at[4], er_sem.at[5], z, 2 * me + h)

    @pl.when(me != z)
    def _():
        swap.start()
        swap.wait()
        gt_out[...] = e3recv[...]

    @pl.when(me == z)
    def _():
        gt_out[...] = e3send[...]

    for k in range(2, 6):
        hidden_copy(k).wait_recv()

    @pl.loop(0, n)
    def _(c):
        hidden_result(c).start()

    for k in range(6):
        hidden_copy(k).wait_send()
    for k in range(1, 4):
        piece(k).wait_send()
    for kind in range(2):
        for block in range(4):
            @pl.when((z >= block) & (z < 3))
            def _(block=block, kind=kind):
                upward(block, kind).wait_send()

            @pl.when((z <= block) & (z > 0))
            def _(block=block, kind=kind):
                downward(block, kind).wait_send()

            @pl.when(block != me)
            def _(block=block, kind=kind):
                to_owner(block, kind).wait_send()

            to_core(block, kind).wait_send()

    @pl.loop(0, n)
    def _(c):
        for copy in results(c):
            copy.wait()
        hidden_result(c).wait()


def fused(tokens, grad_out, w_gate, w_up, w_down):
    rows, feats = tokens.shape
    width, units = w_gate.shape
    chunk = 128
    n, count = units // chunk, 4 * rows
    signs = (hadamard(HB) * math.sqrt(HB)).astype(BF16)
    whole, anywhere = pl.BlockSpec(memory_space=pltpu.VMEM), pl.BlockSpec(memory_space=pl.ANY)
    wide = jax.ShapeDtypeStruct((4, rows, units), BF16)
    turned = [jax.ShapeDtypeStruct(dims, BF16) for dims in ((width, count), (count, width))]
    dma = pltpu.SemaphoreType.DMA
    hidden, d_gate, d_up, grad_tokens, x_turned, dy_turned = pl.pallas_call(
        functools.partial(fused_kernel, n),
        out_shape=(wide, wide, wide, jax.ShapeDtypeStruct((rows, feats), BF16), *turned),
        in_specs=[whole] * 3 + [anywhere] * 3,
        out_specs=(anywhere,) * 3 + (whole,) * 3,
        scratch_shapes=[
            pltpu.VMEM((n, width, 2 * chunk), BF16),
            pltpu.VMEM((n, chunk, width), BF16),
            pltpu.VMEM((2 * LAG + 1, 4, 3, rows, chunk), F32),
            pltpu.VMEM((n, 2, 3, rows, chunk), BF16),
            pltpu.VMEM((n, 2, 3, rows, chunk), BF16),
            pltpu.VMEM((n, 3, rows, chunk), BF16),
            pltpu.VMEM((n, 3, rows, chunk), BF16),
            pltpu.VMEM((n, 4, 2, rows, chunk), BF16),
            pltpu.VMEM((n, 4, rows, chunk), BF16),
            pltpu.VMEM((4, 2, rows, feats), BF16),
            pltpu.VMEM((4, 2, 2, rows, feats), BF16),
            pltpu.VMEM((count, width), BF16),
            pltpu.VMEM((count, width), BF16),
            pltpu.VMEM((count, width), F32),
            pltpu.VMEM((count, feats), F32),
            pltpu.VMEM((4, rows, feats), BF16),
            pltpu.VMEM((4, rows, feats), BF16),
            pltpu.VMEM((rows, feats), BF16),
            pltpu.VMEM((rows, feats), BF16),
            dma((3, n)), dma((3, n)), dma((8, n)), dma((8, n)),
            dma((4, 2, 4)), dma((3, 2, 4)), dma((6,)), dma((6,)), dma((5,)), dma((6,)),
        ],
        compiler_params=pltpu.CompilerParams(
            collective_id=0, has_side_effects=True, vmem_limit_bytes=62 * 2**20
        ),
        cost_estimate=pl.CostEstimate(
            flops=10 * count * width * units, bytes_accessed=12 * width * units, transcendentals=0
        ),
    )(tokens, grad_out, signs, w_gate, w_up, w_down)
    flat = [v.reshape(count, units) for v in (hidden, d_gate, d_up)]
    return (grad_tokens, *gradients(x_turned, dy_turned, *flat))


def gradients_kernel(x_ref, dy_ref, hid_ref, dg_ref, du_ref, gate_ref, up_ref, down_ref):
    gate_ref[...] = jnp.dot(x_ref[...], dg_ref[...], preferred_element_type=F32).astype(BF16)
    up_ref[...] = jnp.dot(x_ref[...], du_ref[...], preferred_element_type=F32).astype(BF16)
    down_ref[...] = dot_dims(hid_ref[...], dy_ref[...], 0, 0).astype(BF16)


def gradients(x_turned, dy_turned, hidden, d_gate, d_up):
    width, count = x_turned.shape
    units = hidden.shape[1]
    tile = 512
    once = [pl.BlockSpec(dims, lambda i: (0, 0)) for dims in ((width, count), (count, width))]
    act = pl.BlockSpec((count, tile), lambda i: (0, i))
    grad = pl.BlockSpec((width, tile), lambda i: (0, i))
    wide = jax.ShapeDtypeStruct((width, units), BF16)
    return pl.pallas_call(
        gradients_kernel,
        grid=(units // tile,),
        out_shape=(wide, wide, jax.ShapeDtypeStruct((units, width), BF16)),
        in_specs=[*once, act, act, act],
        out_specs=(grad, grad, pl.BlockSpec((tile, width), lambda i: (i, 0))),
        compiler_params=pltpu.CompilerParams(vmem_limit_bytes=60 * 2**20),
        cost_estimate=pl.CostEstimate(
            flops=6 * count * width * units, bytes_accessed=12 * width * units, transcendentals=0
        ),
    )(x_turned, dy_turned, hidden, d_gate, d_up)


def plain(n_rep, n_fsdp, tokens, grad_out, w_gate, w_up, w_down):
    x_block, dy_block = gather_blocks(tokens, grad_out)
    hidden, d_gate, d_up, partial = middle_plain(x_block, dy_block, w_gate, w_up, w_down)
    grad_tokens = scatter_tokens(partial, n_rep, n_fsdp)
    x_turned, dy_turned = rotate_features(x_block), rotate_features(dy_block)
    return (
        grad_tokens,
        dot_dims(x_turned, d_gate, 0, 0).astype(BF16),
        dot_dims(x_turned, d_up, 0, 0).astype(BF16),
        dot_dims(hidden, dy_turned, 0, 0).astype(BF16),
    )


def solution(mesh):
    n_rep, n_fsdp = mesh.shape["rep"], mesh.shape["fsdp"]
    body = fused if (n_rep, n_fsdp) == (8, 4) else functools.partial(plain, n_rep, n_fsdp)
    return jax.shard_map(
        body,
        mesh=mesh,
        in_specs=(P("fsdp", "rep"),) * 4 + (P("rep", "fsdp"),),
        out_specs=(P("fsdp", "rep"),) * 3 + (P("rep", "fsdp"),),
        check_vma=False,
    )
```
